32 devices in a mesh: sec: 4 (over x, core), lat: 8 (over z, y).
Axes of the slice: x: 2, y: 2, z: 4, core: 2. Of those that a mesh axis runs over, the one named last changes fastest.
Arguments:
- ocean_state: float32 [24, 128, 1024], P(None, 'lat', 'sec'), may hold values from -6 to 6
- land_mask: int32 [128, 1024], P('lat', 'sec'), may hold values from 0 to 1
- layer_count: int32 [128, 1024], P('lat', 'sec'), may hold values from 1 to 8
- conv1_weight: bfloat16 [5, 128, 120], replicated, may hold values from -1 to 1
- conv1_bias: float32 [128], replicated, may hold values from -3 to 3
- conv2_weight: bfloat16 [5, 64, 640], replicated, may hold values from -1 to 1
- conv2_bias: float32 [64], replicated, may hold values from -3 to 3
- conv3_weight: bfloat16 [5, 32, 320], replicated, may hold values from -1 to 1
- conv3_bias: float32 [32], replicated, may hold values from -3 to 3
- conv4_weight: bfloat16 [5, 16, 160], replicated, may hold values from -1 to 1
Outputs:
- final_state: float32 [24, 128, 1024], P(None, 'lat', 'sec')
- forcing: float32 [16, 128, 1024], P(None, 'lat', 'sec')
The draws below stay inside these ranges and needn't reach their ends.
All inputs are finite; a program needn't handle non-finite values.
Results may differ from the reference program's by a relative error of at most 0.015.
Values may be sent and summed in bfloat16 or wider, within the bound.
A program may use at most 128 MiB of HBM per device.

```python
import jax
import jax.numpy as jnp
from jax import lax

LEVELS = 8
CIN = 24
COUT = 16
H1 = 128
H2 = 64
H3 = 32
STEPS = 4
NY = 128
NX = 1024


def basin_parts(key):
    basin_size = min(NY, NX)
    row_index = lax.broadcasted_iota(jnp.int32, (NY, NX), 0)
    col_index = lax.broadcasted_iota(jnp.int32, (NY, NX), 1)
    centre_rows = jax.random.randint(jax.random.fold_in(key, 11), (8,), 0, NY)
    centre_cols = jax.random.randint(jax.random.fold_in(key, 12), (8,), 0, NX)
    least_radius = max(basin_size // 16, 1)
    radius_all = jax.random.randint(jax.random.fold_in(key, 13), (8,), least_radius, max(basin_size // 4, least_radius + 1))
    shore_gap = jnp.full((NY, NX), 2 ** 30, jnp.int32)
    for continent in range(8):
        row_gap = row_index - centre_rows[continent]
        col_gap = col_index - centre_cols[continent]
        excess = row_gap * row_gap + col_gap * col_gap - radius_all[continent] * radius_all[continent]
        shore_gap = jnp.minimum(shore_gap, excess)
    return (row_index, col_index, shore_gap)


def draw_land_mask(key, part):
    row_index, col_index, shore_gap = basin_parts(jax.random.fold_in(key, 5))
    sea_cells = (shore_gap > 0).astype(jnp.int32)
    corner = (row_index == 0) & (col_index == 0)
    return jnp.where(corner, 1, sea_cells).astype(jnp.int32)


def draw_layer_count(key, part):
    row_index, col_index, shore_gap = basin_parts(jax.random.fold_in(key, 5))
    basin_size = min(NY, NX)
    least_cycle = max(basin_size * basin_size // 256, 1)
    cycle_width = jax.random.randint(jax.random.fold_in(key, 6), (), least_cycle, max(basin_size * basin_size // 16, least_cycle + 1))
    depth_count = jnp.ones((NY, NX), jnp.int32)
    for cycle_number in range(1, LEVELS):
        depth_count = depth_count + (shore_gap > cycle_number * cycle_width).astype(jnp.int32)
    jitter = jax.random.randint(jax.random.fold_in(key, 7), (NY, NX), -1, 2)
    depth_count = jnp.clip(depth_count + jitter, 1, LEVELS)
    depth_count = jnp.where((row_index == 0) & (col_index == 0), LEVELS, depth_count)
    depth_count = jnp.where((row_index == 0) & (col_index == 1), 1, depth_count)
    return depth_count.astype(jnp.int32)


def draw_ocean_state(key, part):
    magnitude = jax.random.uniform(jax.random.fold_in(key, 61), (2 * LEVELS, 1, 1), jnp.float32, 1.5, 2.5)
    flips = jax.random.randint(jax.random.fold_in(key, 62), (2 * LEVELS, 1, 1), 0, 2)
    offset_vel = magnitude * (2 * flips - 1).astype(jnp.float32)
    drift = jnp.concatenate([offset_vel, jnp.zeros((LEVELS, 1, 1), jnp.float32)], axis=0)
    noise = jnp.clip(jax.random.normal(jax.random.fold_in(key, 64), (CIN, NY, NX), jnp.float32), -3.5, 3.5)
    return (noise + drift).astype(jnp.float32)


def kernel_taps(key, out_width, in_width):
    spread = (25.0 * in_width) ** (-0.5)
    taps = jnp.clip(jax.random.normal(jax.random.fold_in(key, 21), (5, out_width, 5, in_width), jnp.float32), -4.0, 4.0)
    common = jnp.clip(jax.random.normal(jax.random.fold_in(key, 22), (1, out_width, 1, in_width), jnp.float32), -3.0, 3.0)
    weight = spread * (taps + 0.35 * common)
    return weight.reshape(5, out_width, 5 * in_width).astype(jnp.bfloat16)


def draw_conv1_weight(key, part):
    return kernel_taps(jax.random.fold_in(key, 31), H1, CIN)


def draw_conv2_weight(key, part):
    return kernel_taps(jax.random.fold_in(key, 41), H2, H1)


def draw_conv3_weight(key, part):
    return kernel_taps(jax.random.fold_in(key, 51), H3, H2)


def draw_conv4_weight(key, part):
    return kernel_taps(jax.random.fold_in(key, 71), COUT, H3)


def gaussian(key, extent, scale, bound, held_as=jnp.bfloat16):
    return jnp.clip(scale * jax.random.normal(key, extent, jnp.float32), -bound, bound).astype(held_as)


def setup_inputs(seed: int = 0) -> dict:
    key_list = jax.random.split(jax.random.key(seed), 11)
    ocean_state = draw_ocean_state(jax.random.fold_in(key_list[10], 71), 0)
    land_mask = draw_land_mask(jax.random.fold_in(key_list[10], 71), 0)
    layer_count = draw_layer_count(jax.random.fold_in(key_list[10], 71), 0)
    conv1_weight = draw_conv1_weight(jax.random.fold_in(key_list[10], 71), 0)
    conv1_bias = gaussian(key_list[4], (H1,), 0.5, 3.0, jnp.float32)
    conv2_weight = draw_conv2_weight(jax.random.fold_in(key_list[10], 71), 0)
    conv2_bias = gaussian(key_list[6], (H2,), 0.5, 3.0, jnp.float32)
    conv3_weight = draw_conv3_weight(jax.random.fold_in(key_list[10], 71), 0)
    conv3_bias = gaussian(key_list[8], (H3,), 0.5, 3.0, jnp.float32)
    conv4_weight = draw_conv4_weight(jax.random.fold_in(key_list[10], 71), 0)
    return {"ocean_state": ocean_state, "land_mask": land_mask, "layer_count": layer_count, "conv1_weight": conv1_weight, "conv1_bias": conv1_bias, "conv2_weight": conv2_weight, "conv2_bias": conv2_bias, "conv3_weight": conv3_weight, "conv3_bias": conv3_bias, "conv4_weight": conv4_weight}


time_step = 0.3
drag_rate = 0.05


def coupling(count_levels):
    row_index = lax.broadcasted_iota(jnp.int32, (count_levels, count_levels), 0)
    col_index = lax.broadcasted_iota(jnp.int32, (count_levels, count_levels), 1)
    return 0.5 + 0.1 * jnp.minimum(row_index, col_index).astype(jnp.float32)


def conv_layer(layer_in, weight):
    out_rows = layer_in.shape[1] - 4
    out_cols = layer_in.shape[2] - 4
    summed = jnp.zeros((weight.shape[1], out_rows, out_cols), jnp.float32)
    for shift_y in range(5):
        row_band = layer_in[:, shift_y:shift_y + out_rows, :]
        stacked = jnp.concatenate([row_band[:, :, shift_x:shift_x + out_cols] for shift_x in range(5)], axis=0)
        summed = summed + jnp.einsum("oc,crx->orx", weight[shift_y], stacked, preferred_element_type=jnp.float32)
    return summed


def ocean_step(padded, wet_pad, forcing, coriolis, coupling_matrix):
    zonal_vel = padded[:LEVELS]
    merid_vel = padded[LEVELS:2 * LEVELS]
    thickness = padded[2 * LEVELS:]
    divergence = (zonal_vel[:, 1:-1, 2:] - zonal_vel[:, 1:-1, :-2]) * 0.5 + (merid_vel[:, 2:, 1:-1] - merid_vel[:, :-2, 1:-1]) * 0.5
    h_cycle = (thickness[:, 1:-1, 1:-1] - time_step * divergence) * wet_pad[:, 1:-1, 1:-1]
    pressure = jnp.einsum("kj,jrx->krx", coupling_matrix, h_cycle, precision=lax.Precision.HIGHEST)
    grad_x = (pressure[:, 1:-1, 2:] - pressure[:, 1:-1, :-2]) * 0.5
    grad_y = (pressure[:, 2:, 1:-1] - pressure[:, :-2, 1:-1]) * 0.5
    zonal_mid = zonal_vel[:, 2:-2, 2:-2]
    merid_mid = merid_vel[:, 2:-2, 2:-2]
    wet_mid = wet_pad[:, 2:-2, 2:-2]
    zonal_new = (zonal_mid + time_step * (-grad_x + coriolis * merid_mid - drag_rate * zonal_mid + forcing[:LEVELS])) * wet_mid
    merid_new = (merid_mid + time_step * (-grad_y - coriolis * zonal_mid - drag_rate * merid_mid + forcing[LEVELS:])) * wet_mid
    return jnp.concatenate([zonal_new, merid_new, h_cycle[:, 1:-1, 1:-1]], axis=0)


def pad_two(field):
    return jnp.pad(field, ((0, 0), (2, 2), (2, 2)))


def reference(ocean_state, land_mask, layer_count, conv1_weight, conv1_bias, conv2_weight, conv2_bias, conv3_weight, conv3_bias, conv4_weight):
    levels = land_mask * layer_count
    wet_mask = (lax.broadcasted_iota(jnp.int32, (LEVELS, NY, NX), 0) < levels[None]).astype(jnp.float32)
    sea_mask = (levels > 0).astype(jnp.float32)[None]
    wet_two = jnp.concatenate([wet_mask, wet_mask], axis=0)
    wet_three = jnp.concatenate([wet_mask, wet_mask, wet_mask], axis=0)
    counts = jnp.maximum(jnp.sum(wet_mask, axis=(1, 2)), 1.0)
    counts_two = jnp.concatenate([counts, counts])
    coriolis = 0.3 + 0.5 * lax.broadcasted_iota(jnp.int32, (1, NY, 1), 1).astype(jnp.float32) / NY
    coupling_matrix = coupling(LEVELS)
    state = ocean_state * wet_three
    forcing = jnp.zeros((2 * LEVELS, NY, NX), jnp.float32)
    for step_index in range(STEPS):
        hidden = state.astype(jnp.bfloat16)
        for weight, offset in ((conv1_weight, conv1_bias), (conv2_weight, conv2_bias), (conv3_weight, conv3_bias)):
            hidden = (jax.nn.silu(conv_layer(pad_two(hidden), weight) + offset[:, None, None]) * sea_mask).astype(jnp.bfloat16)
        raw_forcing = conv_layer(pad_two(hidden), conv4_weight)
        wet_sums = jnp.sum(raw_forcing * wet_two, axis=(1, 2))
        forcing = (raw_forcing - (wet_sums / counts_two)[:, None, None]) * wet_two
        state = ocean_step(pad_two(state), pad_two(wet_mask), forcing, coriolis, coupling_matrix)
    return state, forcing
```

```python
import functools

import jax
import jax.numpy as jnp
from jax import lax
from jax.experimental import pallas as pl
from jax.experimental.pallas import tpu as pltpu
from jax.sharding import PartitionSpec as P

LEVELS = 8
STEPS = 4
HALO = 8
LANES = 128
CHUNK = 512

time_step = 0.3
drag_rate = 0.05

DIRS = ((-1, 0), (1, 0), (-1, -1), (0, -1), (1, -1), (-1, 1), (0, 1), (1, 1))


def round_up(value, unit):
    return (value + unit - 1) // unit * unit


def kernel(
    rows, cols, n_sec, n_lat,
    xin, cor, cmask, w1, b1, w2, b2, w3, b3, w4,
    state_out, forcing_out,
    x, p, a1, a2, a3, raw, rawc, wet, sea,
    send_rows, send_strip, recv_rows, recv_strip, sum_sec, sum_lat, got_sec, got_lat,
    halo_send, halo_recv, sec_send, sec_recv, lat_send, lat_recv,
):
    pitch = cols + 2 * HALO
    full = (rows + 2 * HALO) * pitch
    lo, hi = HALO * pitch, (HALO + rows) * pitch
    mid = hi - lo
    sec = lax.axis_index("sec")
    lat = lax.axis_index("lat")

    exists = []
    for dl, ds in DIRS:
        ok = jnp.bool_(True)
        if dl:
            ok = jnp.logical_and(ok, lat > 0 if dl < 0 else lat < n_lat - 1)
        if ds:
            ok = jnp.logical_and(ok, sec > 0 if ds < 0 else sec < n_sec - 1)
        exists.append(ok)

    def peer(dl, ds):
        return {"sec": sec + ds, "lat": lat + dl}

    barrier = pltpu.get_barrier_semaphore()
    for d in range(1, n_sec):
        pl.semaphore_signal(
            barrier, inc=1, device_id={"sec": lax.rem(sec + d, n_sec), "lat": lat},
            device_id_type=pl.DeviceIdType.MESH,
        )
    for d in range(1, n_lat):
        pl.semaphore_signal(
            barrier, inc=1, device_id={"sec": sec, "lat": lax.rem(lat + d, n_lat)},
            device_id_type=pl.DeviceIdType.MESH,
        )
    for k, (dl, ds) in enumerate(DIRS):
        if dl and ds:

            @pl.when(exists[k])
            def _():
                pl.semaphore_signal(
                    barrier, inc=1, device_id=peer(dl, ds), device_id_type=pl.DeviceIdType.MESH
                )

    x[:, full:] = jnp.zeros((4 * LEVELS, x.shape[1] - full), jnp.float32)
    x[:, lo:hi] = xin[...]
    for k in range(len(DIRS)):

        @pl.when(jnp.logical_not(exists[k]))
        def _():
            for t in range(STEPS):
                if k < 2:
                    recv_rows[t, k] = jnp.zeros(recv_rows.shape[2:], jnp.bfloat16)
                else:
                    recv_strip[t, k - 2] = jnp.zeros(recv_strip.shape[2:], jnp.bfloat16)

    n_diag = jnp.int32(0)
    for k, (dl, ds) in enumerate(DIRS):
        if dl and ds:
            n_diag = n_diag + jnp.where(exists[k], 1, 0)
    pl.semaphore_wait(barrier, n_sec - 1 + n_lat - 1 + n_diag)

    lane = lax.broadcasted_iota(jnp.int32, (4 * LEVELS, LANES), 1)

    def halo_copy(t, k):
        dl, ds = DIRS[k]
        back = DIRS.index((-dl, -ds))
        if ds == 0:
            start = 0 if dl < 0 else mid - HALO * pitch
            src = send_rows.at[t, :, start : start + HALO * pitch]
            dst = recv_rows.at[t, back]
        else:
            src = send_strip.at[t, 0 if ds < 0 else 1]
            dst = recv_strip.at[t, back - 2]
        return pltpu.make_async_remote_copy(
            src_ref=src, dst_ref=dst, send_sem=halo_send.at[t, k], recv_sem=halo_recv.at[t, back],
            device_id=peer(dl, ds), device_id_type=pl.DeviceIdType.MESH,
        )

    def halo_arrival(t, k):
        dl, ds = DIRS[k]
        if ds == 0:
            src, dst = send_rows.at[t, :, 0 : HALO * pitch], recv_rows.at[t, k]
        else:
            src, dst = send_strip.at[t, 0], recv_strip.at[t, k - 2]
        return pltpu.make_async_remote_copy(
            src_ref=src, dst_ref=dst, send_sem=halo_send.at[t, k], recv_sem=halo_recv.at[t, k],
            device_id=peer(dl, ds), device_id_type=pl.DeviceIdType.MESH,
        )

    def start_halo(t):
        send_rows[t] = x[:, lo:hi].astype(jnp.bfloat16)
        for side in range(2):
            packed = jnp.zeros((4 * LEVELS, LANES), jnp.float32)
            for row in range(rows):
                place = (HALO + row) * pitch + (HALO if side == 0 else cols)
                base, off = place // LANES * LANES, place % LANES
                part = x[:, base : base + LANES]
                turn = (HALO * row - off) % LANES
                if turn:
                    part = pltpu.roll(part, turn, 1)
                here = (lane >= HALO * row) & (lane < HALO * (row + 1))
                packed = jnp.where(here, part, packed)
            send_strip[t, side] = packed.astype(jnp.bfloat16)
        for k in range(len(DIRS)):

            @pl.when(exists[k])
            def _():
                halo_copy(t, k).start()

    def finish_halo(t):
        for k in range(len(DIRS)):

            @pl.when(exists[k])
            def _():
                halo_arrival(t, k).wait_recv()
                halo_copy(t, k).wait_send()

        x[:, :lo] = recv_rows[t, 0].astype(jnp.float32)
        x[:, hi:full] = recv_rows[t, 1].astype(jnp.float32)
        for side in range(2):
            strips = [recv_strip[t, 3 * side + j].astype(jnp.float32) for j in range(3)]
            for ext in range(rows + 2 * HALO):
                if ext < HALO:
                    strip, from_row = strips[0], rows - HALO + ext
                elif ext < HALO + rows:
                    strip, from_row = strips[1], ext - HALO
                else:
                    strip, from_row = strips[2], ext - HALO - rows
                place = ext * pitch + (0 if side == 0 else HALO + cols)
                base, off = place // LANES * LANES, place % LANES
                turn = (off - HALO * from_row) % LANES
                if turn:
                    strip = pltpu.roll(strip, turn, 1)
                here = (lane >= off) & (lane < off + HALO)
                x[:, base : base + LANES] = jnp.where(here, strip, x[:, base : base + LANES])

    def total(t, mine):
        for axis, count, held, got, send, recv in (
            ("sec", n_sec, sum_sec, got_sec, sec_send, sec_recv),
            ("lat", n_lat, sum_lat, got_lat, lat_send, lat_recv),
        ):
            held[t] = mine
            copies = []
            for d in range(1, count):
                if axis == "sec":
                    target = {"sec": lax.rem(sec + d, count), "lat": lat}
                else:
                    target = {"sec": sec, "lat": lax.rem(lat + d, count)}
                copies.append(
                    pltpu.make_async_remote_copy(
                        src_ref=held.at[t], dst_ref=got.at[t, d - 1], send_sem=send.at[t, d - 1],
                        recv_sem=recv.at[t, d - 1], device_id=target,
                        device_id_type=pl.DeviceIdType.MESH,
                    )
                )
            for copy in copies:
                copy.start()
            for d, copy in enumerate(copies):
                copy.wait_recv()
                mine = mine + got[t, d]
            for copy in copies:
                copy.wait_send()
        counts = jnp.maximum(mine[2 * LEVELS :], 1.0)
        return (mine[: 2 * LEVELS] / jnp.concatenate([counts, counts], axis=0))[:, :1]

    def at(value, offset):
        size = value.shape[1]
        return pltpu.roll(value, (-offset) % size, 1)

    def shifted(ref, top, count, start, offset, size):
        base = offset // LANES * LANES
        rest = offset - base
        if rest == 0:
            return ref[top : top + count, pl.ds(pl.multiple_of(start + base, LANES), size)]
        wide = ref[top : top + count, pl.ds(pl.multiple_of(start + base, LANES), size + LANES)]
        return at(wide, rest)[:, :size]

    def conv(source, channels, weight, row_taps, groups, in_lanes, out_lanes, finish):
        out_channels = weight.shape[0] // groups

        def products(i, carry):
            start = i * CHUNK
            parts = [
                shifted(source, 0, channels, start, tap * pitch + s, CHUNK)
                for tap in range(row_taps)
                for s in range(5)
            ]
            stacked = jnp.concatenate(parts, axis=0).astype(jnp.bfloat16)
            p[: weight.shape[0], pl.ds(pl.multiple_of(start, LANES), CHUNK)] = jnp.dot(
                weight[...], stacked, preferred_element_type=jnp.float32
            )
            return carry

        lax.fori_loop(0, round_up(in_lanes, CHUNK) // CHUNK, products, 0)

        def reduce(i, carry):
            start = i * CHUNK
            summed = shifted(p, 0, out_channels, start, 0, CHUNK)
            for g in range(1, groups):
                summed = summed + shifted(
                    p, g * out_channels, out_channels, start, g * row_taps * pitch, CHUNK
                )
            finish(start, summed)
            return carry

        lax.fori_loop(0, round_up(out_lanes, CHUNK) // CHUNK, reduce, 0)

    def activate(layer, target, bias):
        def finish(start, summed):
            here = pl.ds(pl.multiple_of(start, LANES), CHUNK)
            value = summed + bias[...]
            half = 0.5 * value
            target[:, here] = (half + half * jnp.tanh(half)) * sea[layer, :1, here]

        return finish

    def store_raw(start, summed):
        raw[:, pl.ds(pl.multiple_of(start, LANES), CHUNK)] = summed

    def step(t, mine):
        start_halo(t)
        mean = total(t, mine)
        finish_halo(t)

        @pl.when(t == 0)
        def _():
            levels = x[3 * LEVELS :, :full]
            index = lax.broadcasted_iota(jnp.int32, (LEVELS, full), 0).astype(jnp.float32)
            wet[...] = jnp.where(index < levels, 1.0, 0.0)
            sea_here = jnp.where(levels > 0, 1.0, 0.0)
            for layer in range(3):
                sea[layer, :, :full] = at(sea_here, (layer + 1) * (2 * pitch + 2))

        for f in range(2):
            part = slice(f * LEVELS, (f + 1) * LEVELS)
            x[part, :full] = (x[part, :full] - time_step * mean[part]) * wet[...]
        x[2 * LEVELS : 3 * LEVELS, :full] = x[2 * LEVELS : 3 * LEVELS, :full] * wet[...]

        lanes = [(rows + 4 * j) * pitch for j in range(4, -1, -1)]
        conv(x, 3 * LEVELS, w1, 2, 3, lanes[0], lanes[1], activate(0, a1, b1))
        conv(a1, a1.shape[0], w2, 1, 5, lanes[1], lanes[2], activate(1, a2, b2))
        conv(a2, a2.shape[0], w3, 1, 5, lanes[2], lanes[3], activate(2, a3, b3))
        conv(a3, a3.shape[0], w4, 1, 5, lanes[3], lanes[4], store_raw)

        zonal, merid = x[:LEVELS, :full], x[LEVELS : 2 * LEVELS, :full]
        divergence = (at(zonal, 1) - at(zonal, -1)) * 0.5 + (
            at(merid, pitch) - at(merid, -pitch)
        ) * 0.5
        thick = (x[2 * LEVELS : 3 * LEVELS, :full] - time_step * divergence) * wet[...]
        level = lax.broadcasted_iota(jnp.int32, (LEVELS, 1), 0)
        pressure = jnp.zeros((LEVELS, full), jnp.float32)
        for j in range(LEVELS):
            coef = 0.5 + 0.1 * jnp.minimum(level, j).astype(jnp.float32)
            pressure = pressure + coef * thick[j : j + 1]
        grad_x = ((at(pressure, 1) - at(pressure, -1)) * 0.5)[:, lo:hi]
        grad_y = ((at(pressure, pitch) - at(pressure, -pitch)) * 0.5)[:, lo:hi]
        wet_mid = wet[:, lo:hi]
        zonal, merid = zonal[:, lo:hi], merid[:, lo:hi]
        inside = cmask[...] > 0.0
        raw_u = jnp.where(inside, pltpu.roll(raw[:LEVELS, :mid], HALO, 1), 0.0)
        raw_v = jnp.where(inside, pltpu.roll(raw[LEVELS:, :mid], HALO, 1), 0.0)
        rawc[:LEVELS] = raw_u
        rawc[LEVELS:] = raw_v
        x[:LEVELS, lo:hi] = (
            zonal + time_step * (-grad_x + cor[...] * merid - drag_rate * zonal + raw_u)
        ) * wet_mid
        x[LEVELS : 2 * LEVELS, lo:hi] = (
            merid + time_step * (-grad_y - cor[...] * zonal - drag_rate * merid + raw_v)
        ) * wet_mid
        x[2 * LEVELS : 3 * LEVELS, lo:hi] = thick[:, lo:hi]
        wet_in = jnp.where(inside, wet_mid, 0.0)
        sums = jnp.concatenate(
            [
                jnp.sum(raw_u * wet_in, axis=1, keepdims=True),
                jnp.sum(raw_v * wet_in, axis=1, keepdims=True),
                jnp.sum(wet_in, axis=1, keepdims=True),
            ],
            axis=0,
        )
        return jnp.broadcast_to(sums, (3 * LEVELS, LANES))

    mine = lax.fori_loop(0, STEPS, step, jnp.zeros((3 * LEVELS, LANES), jnp.float32))
    mean = total(STEPS, mine)
    wet_mid = wet[:, lo:hi]
    for f in range(2):
        part = slice(f * LEVELS, (f + 1) * LEVELS)
        state_out[part] = (x[part, lo:hi] - time_step * mean[part]) * wet_mid
        forcing_out[part] = (rawc[part] - mean[part]) * wet_mid
    state_out[2 * LEVELS :] = x[2 * LEVELS : 3 * LEVELS, lo:hi]


def local(
    ocean_state, land_mask, layer_count,
    conv1_weight, conv1_bias, conv2_weight, conv2_bias, conv3_weight, conv3_bias, conv4_weight,
):
    rows, cols = ocean_state.shape[1:]
    n_sec, n_lat = lax.axis_size("sec"), lax.axis_size("lat")
    pitch = cols + 2 * HALO
    full = (rows + 2 * HALO) * pitch
    mid = rows * pitch
    levels = (land_mask * layer_count).astype(jnp.float32)
    fields = jnp.concatenate(
        [ocean_state, jnp.broadcast_to(levels[None], (LEVELS, rows, cols))], axis=0
    )
    xin = jnp.pad(fields, ((0, 0), (0, 0), (HALO, HALO))).reshape(4 * LEVELS, mid)
    row = lax.broadcasted_iota(jnp.int32, (LEVELS, rows, pitch), 1)
    col = lax.broadcasted_iota(jnp.int32, (LEVELS, rows, pitch), 2)
    global_row = (lax.axis_index("lat") * rows + row).astype(jnp.float32)
    cor = (0.3 + 0.5 * global_row / (n_lat * rows)).reshape(LEVELS, mid)
    cmask = ((col >= HALO) & (col < HALO + cols)).astype(jnp.float32).reshape(LEVELS, mid)

    h1, h2, h3 = conv1_weight.shape[1], conv2_weight.shape[1], conv3_weight.shape[1]
    wide = conv1_weight.shape[2]
    w1 = jnp.pad(conv1_weight, ((0, 1), (0, 0), (0, 0))).reshape(3, 2, h1, wide)
    w1 = w1.transpose(0, 2, 1, 3).reshape(3 * h1, 2 * wide)
    w2 = conv2_weight.reshape(-1, conv2_weight.shape[2])
    w3 = conv3_weight.reshape(-1, conv3_weight.shape[2])
    w4 = conv4_weight.reshape(-1, conv4_weight.shape[2])

    room = round_up(full, CHUNK) + CHUNK
    length = [round_up((rows + 4 * j) * pitch, CHUNK) + LANES for j in (3, 2, 1)]
    most = max(w1.shape[0], w2.shape[0], w3.shape[0], w4.shape[0])
    bf, f32 = jnp.bfloat16, jnp.float32
    sums = (STEPS + 1, 3 * LEVELS, LANES)
    vmem = pl.BlockSpec(memory_space=pltpu.VMEM)
    state, forcing = pl.pallas_call(
        functools.partial(kernel, rows, cols, n_sec, n_lat),
        out_shape=(
            jax.ShapeDtypeStruct((3 * LEVELS, mid), f32),
            jax.ShapeDtypeStruct((2 * LEVELS, mid), f32),
        ),
        in_specs=[vmem] * 10,
        out_specs=(vmem, vmem),
        scratch_shapes=[
            pltpu.VMEM((4 * LEVELS, room), f32),
            pltpu.VMEM((most, room + 2 * CHUNK), f32),
            pltpu.VMEM((h1, length[0]), f32),
            pltpu.VMEM((h2, length[1]), f32),
            pltpu.VMEM((h3, length[2]), f32),
            pltpu.VMEM((2 * LEVELS, round_up(mid, CHUNK)), f32),
            pltpu.VMEM((2 * LEVELS, mid), f32),
            pltpu.VMEM((LEVELS, full), f32),
            pltpu.VMEM((3, LEVELS, room), f32),
            pltpu.VMEM((STEPS, 4 * LEVELS, mid), bf),
            pltpu.VMEM((STEPS, 2, 4 * LEVELS, LANES), bf),
            pltpu.VMEM((STEPS, 2, 4 * LEVELS, HALO * pitch), bf),
            pltpu.VMEM((STEPS, 6, 4 * LEVELS, LANES), bf),
            pltpu.VMEM(sums, f32),
            pltpu.VMEM(sums, f32),
            pltpu.VMEM((STEPS + 1, n_sec - 1) + sums[1:], f32),
            pltpu.VMEM((STEPS + 1, n_lat - 1) + sums[1:], f32),
            pltpu.SemaphoreType.DMA((STEPS, len(DIRS))),
            pltpu.SemaphoreType.DMA((STEPS, len(DIRS))),
            pltpu.SemaphoreType.DMA((STEPS + 1, n_sec - 1)),
            pltpu.SemaphoreType.DMA((STEPS + 1, n_sec - 1)),
            pltpu.SemaphoreType.DMA((STEPS + 1, n_lat - 1)),
            pltpu.SemaphoreType.DMA((STEPS + 1, n_lat - 1)),
        ],
        compiler_params=pltpu.CompilerParams(
            collective_id=0, has_side_effects=True, vmem_limit_bytes=56 * 2**20
        ),
    )(
        xin, cor, cmask,
        w1, conv1_bias[:, None], w2, conv2_bias[:, None], w3, conv3_bias[:, None], w4,
    )

    def block(flat):
        return flat.reshape(-1, rows, pitch)[:, :, HALO : HALO + cols]

    return (block(state), block(forcing))


def solution(mesh):
    return jax.shard_map(
        local,
        mesh=mesh,
        in_specs=(
            P(None, "lat", "sec"), P("lat", "sec"), P("lat", "sec"),
            P(), P(), P(), P(), P(), P(), P(),
        ),
        out_specs=(P(None, "lat", "sec"), P(None, "lat", "sec")),
        check_vma=False,
    )
```

```python
import functools

import jax
import jax.numpy as jnp
from jax import lax
from jax.experimental import pallas as pl
from jax.experimental.pallas import tpu as pltpu
from jax.sharding import PartitionSpec as P

LEVELS = 8
STEPS = 4
HALO = 8
LANES = 128
CHUNK = 512

time_step = 0.3
drag_rate = 0.05

DIRS = ((-1, 0), (1, 0), (-1, -1), (0, -1), (1, -1), (-1, 1), (0, 1), (1, 1))


def round_up(value, unit):
    return (value + unit - 1) // unit * unit


def kernel(
    rows, cols, n_sec, n_lat,
    xin, cor, cmask, w1_wide, b1, w2_wide, b2, w3_wide, b3, w4_wide,
    state_out, forcing_out,
    x, a1, a2, a3, s1, s2, s3, s4, w1, w2, w3, w4, raw, rawc, wet, sea,
    send_rows, send_strip, recv_rows, recv_strip, sum_sec, sum_lat, got_sec, got_lat,
    halo_send, halo_recv, sec_send, sec_recv, lat_send, lat_recv,
):
    pitch = cols + 2 * HALO
    full = (rows + 2 * HALO) * pitch
    lo, hi = HALO * pitch, (HALO + rows) * pitch
    mid = hi - lo
    sec = lax.axis_index("sec")
    lat = lax.axis_index("lat")

    exists = []
    for dl, ds in DIRS:
        ok = jnp.bool_(True)
        if dl:
            ok = jnp.logical_and(ok, lat > 0 if dl < 0 else lat < n_lat - 1)
        if ds:
            ok = jnp.logical_and(ok, sec > 0 if ds < 0 else sec < n_sec - 1)
        exists.append(ok)

    def peer(dl, ds):
        return {"sec": sec + ds, "lat": lat + dl}

    barrier = pltpu.get_barrier_semaphore()
    for d in range(1, n_sec):
        pl.semaphore_signal(
            barrier, inc=1, device_id={"sec": lax.rem(sec + d, n_sec), "lat": lat},
            device_id_type=pl.DeviceIdType.MESH,
        )
    for d in range(1, n_lat):
        pl.semaphore_signal(
            barrier, inc=1, device_id={"sec": sec, "lat": lax.rem(lat + d, n_lat)},
            device_id_type=pl.DeviceIdType.MESH,
        )
    for k, (dl, ds) in enumerate(DIRS):
        if dl and ds:

            @pl.when(exists[k])
            def _():
                pl.semaphore_signal(
                    barrier, inc=1, device_id=peer(dl, ds), device_id_type=pl.DeviceIdType.MESH
                )

    x[:, full:] = jnp.zeros((4 * LEVELS, x.shape[1] - full), jnp.float32)
    x[:, lo:hi] = xin[...]
    for k in range(len(DIRS)):

        @pl.when(jnp.logical_not(exists[k]))
        def _():
            for t in range(STEPS):
                if k < 2:
                    recv_rows[t, k] = jnp.zeros(recv_rows.shape[2:], jnp.bfloat16)
                else:
                    recv_strip[t, k - 2] = jnp.zeros(recv_strip.shape[2:], jnp.bfloat16)

    n_diag = jnp.int32(0)
    for k, (dl, ds) in enumerate(DIRS):
        if dl and ds:
            n_diag = n_diag + jnp.where(exists[k], 1, 0)
    pl.semaphore_wait(barrier, n_sec - 1 + n_lat - 1 + n_diag)

    lane = lax.broadcasted_iota(jnp.int32, (4 * LEVELS, LANES), 1)

    def halo_copy(t, k):
        dl, ds = DIRS[k]
        back = DIRS.index((-dl, -ds))
        if ds == 0:
            start = 0 if dl < 0 else mid - HALO * pitch
            src = send_rows.at[t, :, start : start + HALO * pitch]
            dst = recv_rows.at[t, back]
        else:
            src = send_strip.at[t, 0 if ds < 0 else 1]
            dst = recv_strip.at[t, back - 2]
        return pltpu.make_async_remote_copy(
            src_ref=src, dst_ref=dst, send_sem=halo_send.at[t, k], recv_sem=halo_recv.at[t, back],
            device_id=peer(dl, ds), device_id_type=pl.DeviceIdType.MESH,
        )

    def halo_arrival(t, k):
        dl, ds = DIRS[k]
        if ds == 0:
            src, dst = send_rows.at[t, :, 0 : HALO * pitch], recv_rows.at[t, k]
        else:
            src, dst = send_strip.at[t, 0], recv_strip.at[t, k - 2]
        return pltpu.make_async_remote_copy(
            src_ref=src, dst_ref=dst, send_sem=halo_send.at[t, k], recv_sem=halo_recv.at[t, k],
            device_id=peer(dl, ds), device_id_type=pl.DeviceIdType.MESH,
        )

    def start_halo(t):
        send_rows[t] = x[:, lo:hi].astype(jnp.bfloat16)
        for side in range(2):
            packed = jnp.zeros((4 * LEVELS, LANES), jnp.float32)
            for row in range(rows):
                place = (HALO + row) * pitch + (HALO if side == 0 else cols)
                base, off = place // LANES * LANES, place % LANES
                part = x[:, base : base + LANES]
                turn = (HALO * row - off) % LANES
                if turn:
                    part = pltpu.roll(part, turn, 1)
                here = (lane >= HALO * row) & (lane < HALO * (row + 1))
                packed = jnp.where(here, part, packed)
            send_strip[t, side] = packed.astype(jnp.bfloat16)
        for k in range(len(DIRS)):

            @pl.when(exists[k])
            def _():
                halo_copy(t, k).start()

    def finish_halo(t):
        for k in range(len(DIRS)):

            @pl.when(exists[k])
            def _():
                halo_arrival(t, k).wait_recv()
                halo_copy(t, k).wait_send()

        x[:, :lo] = recv_rows[t, 0].astype(jnp.float32)
        x[:, hi:full] = recv_rows[t, 1].astype(jnp.float32)
        for side in range(2):
            strips = [recv_strip[t, 3 * side + j].astype(jnp.float32) for j in range(3)]
            for ext in range(rows + 2 * HALO):
                if ext < HALO:
                    strip, from_row = strips[0], rows - HALO + ext
                elif ext < HALO + rows:
                    strip, from_row = strips[1], ext - HALO
                else:
                    strip, from_row = strips[2], ext - HALO - rows
                place = ext * pitch + (0 if side == 0 else HALO + cols)
                base, off = place // LANES * LANES, place % LANES
                turn = (off - HALO * from_row) % LANES
                if turn:
                    strip = pltpu.roll(strip, turn, 1)
                here = (lane >= off) & (lane < off + HALO)
                x[:, base : base + LANES] = jnp.where(here, strip, x[:, base : base + LANES])

    def total(t, mine):
        for axis, count, held, got, send, recv in (
            ("sec", n_sec, sum_sec, got_sec, sec_send, sec_recv),
            ("lat", n_lat, sum_lat, got_lat, lat_send, lat_recv),
        ):
            held[t] = mine
            copies = []
            for d in range(1, count):
                if axis == "sec":
                    target = {"sec": lax.rem(sec + d, count), "lat": lat}
                else:
                    target = {"sec": sec, "lat": lax.rem(lat + d, count)}
                copies.append(
                    pltpu.make_async_remote_copy(
                        src_ref=held.at[t], dst_ref=got.at[t, d - 1], send_sem=send.at[t, d - 1],
                        recv_sem=recv.at[t, d - 1], device_id=target,
                        device_id_type=pl.DeviceIdType.MESH,
                    )
                )
            for copy in copies:
                copy.start()
            for d, copy in enumerate(copies):
                copy.wait_recv()
                mine = mine + got[t, d]
            for copy in copies:
                copy.wait_send()
        counts = jnp.maximum(mine[2 * LEVELS :], 1.0)
        return (mine[: 2 * LEVELS] / jnp.concatenate([counts, counts], axis=0))[:, :1]

    def at(value, offset):
        size = value.shape[1]
        return pltpu.roll(value, (-offset) % size, 1)

    def shifted(ref, count, start, offset, size):
        if offset == 0:
            return ref[:count, pl.ds(pl.multiple_of(start, LANES), size)]
        wide = ref[:count, pl.ds(pl.multiple_of(start, LANES), size + LANES)]
        return at(wide, offset)[:, :size]

    def band(wide, target, depth, width):
        group = target.shape[1] // width
        target[...] = jnp.zeros(target.shape, target.dtype)
        for j in range(group):
            here = slice(j * width, (j + 1) * width)
            for r in range(5):
                q = j + r
                target[q * depth : (q + 1) * depth, here] = wide[r * depth : (r + 1) * depth, here]

    def cells(row, offset=0, count=pitch):
        start = pl.multiple_of(row * pitch, 16)
        return pl.ds(start + offset if offset else start, count)

    def product(source, weight, row):
        depth = source.shape[1]
        parts = [source[cells(row + q), :] for q in range(weight.shape[0] // depth)]
        return jnp.dot(
            jnp.concatenate(parts, axis=1), weight[...], preferred_element_type=jnp.float32
        )

    def silu(value):
        half = 0.5 * value
        return half + half * jnp.tanh(half)

    def sea_row(layer, row):
        return sea[cells(row + 2 * layer, 2 * layer), :]

    lane_of = lax.broadcasted_iota(jnp.int32, (pitch, LANES), 1)

    def network():
        def gather1(i, carry):
            start = i * CHUNK
            parts = [shifted(x, 3 * LEVELS, start, s, CHUNK) for s in range(5)]
            parts.append(jnp.zeros((LANES - 15 * LEVELS, CHUNK), jnp.float32))
            stacked = jnp.concatenate(parts, axis=0)
            s1[pl.ds(pl.multiple_of(start, LANES), CHUNK), :] = stacked.T.astype(jnp.bfloat16)
            return carry

        lax.fori_loop(0, s1.shape[0] // CHUNK, gather1, 0)

        def conv1(g, carry):
            row = 2 * g
            value = silu(product(s1, w1, row) + b1[...])
            for j in range(2):
                a1[cells(row + j), :] = value[:, j * LANES : (j + 1) * LANES] * sea_row(1, row + j)
            return carry

        lax.fori_loop(0, (rows + 12) // 2, conv1, 0)

        def gather2(row, carry):
            for s in range(5):
                s2[cells(row), s * LANES : (s + 1) * LANES] = a1[cells(row, s), :].astype(
                    jnp.bfloat16
                )
            return carry

        lax.fori_loop(0, rows + 12, gather2, 0)

        def conv2(g, carry):
            row = 4 * g
            value = silu(product(s2, w2, row) + b2[...])
            low = lane_of < LANES // 2
            for k in range(2):
                both = value[:, k * LANES : (k + 1) * LANES]
                turned = pltpu.roll(both, LANES // 2, 1)
                first, second = row + 2 * k, row + 2 * k + 1
                a2[cells(first), :] = jnp.where(low, both, turned) * sea_row(2, first)
                a2[cells(second), :] = jnp.where(low, turned, both) * sea_row(2, second)
            return carry

        lax.fori_loop(0, (rows + 8) // 4, conv2, 0)

        def gather3(row, carry):
            low = lane_of < LANES // 2
            taps = [a2[cells(row, s), :] for s in range(5)]
            pieces = [
                jnp.where(low, taps[0], taps[1]), jnp.where(low, taps[2], taps[3]), taps[4],
            ]
            for k, piece in enumerate(pieces):
                s3[cells(row), k * LANES : (k + 1) * LANES] = piece.astype(jnp.bfloat16)
            return carry

        lax.fori_loop(0, rows + 8, gather3, 0)

        def conv3(g, carry):
            row = 4 * g
            value = silu(product(s3, w3, row) + b3[...])
            for j in range(4):
                mine = (lane_of >= 32 * j) & (lane_of < 32 * (j + 1))
                one = jnp.where(mine, value, 0.0)
                two = one + pltpu.roll(one, 32, 1)
                four = two + pltpu.roll(two, 64, 1)
                a3[cells(row + j), :] = four * sea_row(3, row + j)
            return carry

        lax.fori_loop(0, (rows + 4) // 4, conv3, 0)

        def gather4(row, carry):
            taps = [a3[cells(row, s), :] for s in range(5)]
            piece = taps[3]
            for j in range(3):
                piece = jnp.where((lane_of >= 32 * j) & (lane_of < 32 * (j + 1)), taps[j], piece)
            s4[cells(row), :LANES] = piece.astype(jnp.bfloat16)
            s4[cells(row), LANES:] = taps[4].astype(jnp.bfloat16)
            return carry

        lax.fori_loop(0, rows + 4, gather4, 0)

        value = product(s4, w4, 0)
        tall = round_up(pitch, LANES)
        value = jnp.concatenate(
            [value, jnp.zeros((tall - pitch, value.shape[1]), jnp.float32)], axis=0
        ).T
        spot = lax.broadcasted_iota(jnp.int32, (2 * LEVELS, tall), 1)
        for row in range(rows):
            place = row * pitch + HALO
            base, off = place // LANES * LANES, place % LANES
            part = value[row * 2 * LEVELS : (row + 1) * 2 * LEVELS]
            if off:
                part = pltpu.roll(part, off, 1)
            here = (spot >= off) & (spot < off + cols)
            raw[:, base : base + tall] = jnp.where(here, part, raw[:, base : base + tall])

    band(w1_wide, w1, LANES, LANES)
    band(w2_wide, w2, 5 * LANES, LANES // 2)
    band(w3_wide, w3, 3 * LANES, LANES // 4)
    band(w4_wide, w4, 2 * LANES, 2 * LEVELS)
    raw[...] = jnp.zeros(raw.shape, jnp.float32)

    def step(t, mine):
        start_halo(t)
        mean = total(t, mine)
        finish_halo(t)

        @pl.when(t == 0)
        def _():
            levels = x[3 * LEVELS :, :full]
            index = lax.broadcasted_iota(jnp.int32, (LEVELS, full), 0).astype(jnp.float32)
            wet[...] = jnp.where(index < levels, 1.0, 0.0)
            sea_here = jnp.where(levels > 0, 1.0, 0.0)
            for start in range(0, full, LANES):
                tile = jnp.concatenate([sea_here[:, start : start + LANES]] * 16, axis=0)
                sea[start : start + LANES, :] = tile.T

        for f in range(2):
            part = slice(f * LEVELS, (f + 1) * LEVELS)
            x[part, :full] = (x[part, :full] - time_step * mean[part]) * wet[...]
        x[2 * LEVELS : 3 * LEVELS, :full] = x[2 * LEVELS : 3 * LEVELS, :full] * wet[...]

        network()

        zonal, merid = x[:LEVELS, :full], x[LEVELS : 2 * LEVELS, :full]
        divergence = (at(zonal, 1) - at(zonal, -1)) * 0.5 + (
            at(merid, pitch) - at(merid, -pitch)
        ) * 0.5
        thick = (x[2 * LEVELS : 3 * LEVELS, :full] - time_step * divergence) * wet[...]
        level = lax.broadcasted_iota(jnp.int32, (LEVELS, 1), 0)
        pressure = jnp.zeros((LEVELS, full), jnp.float32)
        for j in range(LEVELS):
            coef = 0.5 + 0.1 * jnp.minimum(level, j).astype(jnp.float32)
            pressure = pressure + coef * thick[j : j + 1]
        grad_x = ((at(pressure, 1) - at(pressure, -1)) * 0.5)[:, lo:hi]
        grad_y = ((at(pressure, pitch) - at(pressure, -pitch)) * 0.5)[:, lo:hi]
        wet_mid = wet[:, lo:hi]
        zonal, merid = zonal[:, lo:hi], merid[:, lo:hi]
        inside = cmask[...] > 0.0
        raw_u = jnp.where(inside, raw[:LEVELS, :mid], 0.0)
        raw_v = jnp.where(inside, raw[LEVELS:, :mid], 0.0)
        rawc[:LEVELS] = raw_u
        rawc[LEVELS:] = raw_v
        x[:LEVELS, lo:hi] = (
            zonal + time_step * (-grad_x + cor[...] * merid - drag_rate * zonal + raw_u)
        ) * wet_mid
        x[LEVELS : 2 * LEVELS, lo:hi] = (
            merid + time_step * (-grad_y - cor[...] * zonal - drag_rate * merid + raw_v)
        ) * wet_mid
        x[2 * LEVELS : 3 * LEVELS, lo:hi] = thick[:, lo:hi]
        wet_in = jnp.where(inside, wet_mid, 0.0)
        sums = jnp.concatenate(
            [
                jnp.sum(raw_u * wet_in, axis=1, keepdims=True),
                jnp.sum(raw_v * wet_in, axis=1, keepdims=True),
                jnp.sum(wet_in, axis=1, keepdims=True),
            ],
            axis=0,
        )
        return jnp.broadcast_to(sums, (3 * LEVELS, LANES))

    mine = lax.fori_loop(0, STEPS, step, jnp.zeros((3 * LEVELS, LANES), jnp.float32))
    mean = total(STEPS, mine)
    wet_mid = wet[:, lo:hi]
    for f in range(2):
        part = slice(f * LEVELS, (f + 1) * LEVELS)
        state_out[part] = (x[part, lo:hi] - time_step * mean[part]) * wet_mid
        forcing_out[part] = (rawc[part] - mean[part]) * wet_mid
    state_out[2 * LEVELS :] = x[2 * LEVELS : 3 * LEVELS, lo:hi]


def local(
    ocean_state, land_mask, layer_count,
    conv1_weight, conv1_bias, conv2_weight, conv2_bias, conv3_weight, conv3_bias, conv4_weight,
):
    rows, cols = ocean_state.shape[1:]
    n_sec, n_lat = lax.axis_size("sec"), lax.axis_size("lat")
    pitch = cols + 2 * HALO
    full = (rows + 2 * HALO) * pitch
    mid = rows * pitch
    levels = (land_mask * layer_count).astype(jnp.float32)
    fields = jnp.concatenate(
        [ocean_state, jnp.broadcast_to(levels[None], (LEVELS, rows, cols))], axis=0
    )
    xin = jnp.pad(fields, ((0, 0), (0, 0), (HALO, HALO))).reshape(4 * LEVELS, mid)
    row = lax.broadcasted_iota(jnp.int32, (LEVELS, rows, pitch), 1)
    col = lax.broadcasted_iota(jnp.int32, (LEVELS, rows, pitch), 2)
    global_row = (lax.axis_index("lat") * rows + row).astype(jnp.float32)
    cor = (0.3 + 0.5 * global_row / (n_lat * rows)).reshape(LEVELS, mid)
    cmask = ((col >= HALO) & (col < HALO + cols)).astype(jnp.float32).reshape(LEVELS, mid)

    def widened(weight, depth, copies):
        turned = weight.transpose(0, 2, 1)
        turned = jnp.pad(turned, ((0, 0), (0, depth - turned.shape[1]), (0, 0)))
        return jnp.tile(turned.reshape(5 * depth, -1), (1, copies))

    w1 = widened(conv1_weight, LANES, 2)
    w2 = widened(conv2_weight, 5 * LANES, 4)
    w3 = widened(conv3_weight, 3 * LANES, 4)
    w4 = widened(conv4_weight, 2 * LANES, rows)
    b1 = jnp.tile(conv1_bias, 2)[None]
    b2 = jnp.tile(conv2_bias, 4)[None]
    b3 = jnp.tile(conv3_bias, 4)[None]
    room = round_up(full, CHUNK) + CHUNK
    bf, f32 = jnp.bfloat16, jnp.float32
    sums = (STEPS + 1, 3 * LEVELS, LANES)
    vmem = pl.BlockSpec(memory_space=pltpu.VMEM)
    state, forcing = pl.pallas_call(
        functools.partial(kernel, rows, cols, n_sec, n_lat),
        out_shape=(
            jax.ShapeDtypeStruct((3 * LEVELS, mid), f32),
            jax.ShapeDtypeStruct((2 * LEVELS, mid), f32),
        ),
        in_specs=[vmem] * 10,
        out_specs=(vmem, vmem),
        scratch_shapes=[
            pltpu.VMEM((4 * LEVELS, room), f32),
            pltpu.VMEM(((rows + 12) * pitch + HALO, LANES), f32),
            pltpu.VMEM(((rows + 8) * pitch + HALO, LANES), f32),
            pltpu.VMEM(((rows + 4) * pitch + HALO, LANES), f32),
            pltpu.VMEM((round_up(full, CHUNK), LANES), bf),
            pltpu.VMEM(((rows + 12) * pitch, 5 * LANES), bf),
            pltpu.VMEM(((rows + 8) * pitch, 3 * LANES), bf),
            pltpu.VMEM(((rows + 4) * pitch, 2 * LANES), bf),
            pltpu.VMEM((6 * LANES, 2 * LANES), bf),
            pltpu.VMEM((8 * 5 * LANES, 2 * LANES), bf),
            pltpu.VMEM((8 * 3 * LANES, LANES), bf),
            pltpu.VMEM(((rows + 4) * 2 * LANES, rows * 2 * LEVELS), bf),
            pltpu.VMEM((2 * LEVELS, mid), f32),
            pltpu.VMEM((2 * LEVELS, mid), f32),
            pltpu.VMEM((LEVELS, full), f32),
            pltpu.VMEM((full, LANES), f32),
            pltpu.VMEM((STEPS, 4 * LEVELS, mid), bf),
            pltpu.VMEM((STEPS, 2, 4 * LEVELS, LANES), bf),
            pltpu.VMEM((STEPS, 2, 4 * LEVELS, HALO * pitch), bf),
            pltpu.VMEM((STEPS, 6, 4 * LEVELS, LANES), bf),
            pltpu.VMEM(sums, f32),
            pltpu.VMEM(sums, f32),
            pltpu.VMEM((STEPS + 1, n_sec - 1) + sums[1:], f32),
            pltpu.VMEM((STEPS + 1, n_lat - 1) + sums[1:], f32),
            pltpu.SemaphoreType.DMA((STEPS, len(DIRS))),
            pltpu.SemaphoreType.DMA((STEPS, len(DIRS))),
            pltpu.SemaphoreType.DMA((STEPS + 1, n_sec - 1)),
            pltpu.SemaphoreType.DMA((STEPS + 1, n_sec - 1)),
            pltpu.SemaphoreType.DMA((STEPS + 1, n_lat - 1)),
            pltpu.SemaphoreType.DMA((STEPS + 1, n_lat - 1)),
        ],
        compiler_params=pltpu.CompilerParams(
            collective_id=0, has_side_effects=True, vmem_limit_bytes=60 * 2**20
        ),
    )(
        xin, cor, cmask,
        w1, b1, w2, b2, w3, b3, w4,
    )

    def block(flat):
        return flat.reshape(-1, rows, pitch)[:, :, HALO : HALO + cols]

    return (block(state), block(forcing))


def solution(mesh):
    return jax.shard_map(
        local,
        mesh=mesh,
        in_specs=(
            P(None, "lat", "sec"), P("lat", "sec"), P("lat", "sec"),
            P(), P(), P(), P(), P(), P(), P(),
        ),
        out_specs=(P(None, "lat", "sec"), P(None, "lat", "sec")),
        check_vma=False,
    )
```

```python
import functools

import jax
import jax.numpy as jnp
from jax import lax
from jax.experimental import pallas as pl
from jax.experimental.pallas import tpu as pltpu
from jax.sharding import PartitionSpec as P

LEVELS = 8
STEPS = 4
HALO = 8
LANES = 128
CHUNK = 512

time_step = 0.3
drag_rate = 0.05

DIRS = ((-1, 0), (1, 0), (-1, -1), (0, -1), (1, -1), (-1, 1), (0, 1), (1, 1))


def round_up(value, unit):
    return (value + unit - 1) // unit * unit


def kernel(
    rows, cols, n_sec, n_lat,
    xin, w1_wide, b1, w2_wide, b2, w3_wide, b3, w4_wide,
    state_out, forcing_out,
    x, a1, a2, a3, s1, s2, s3, s4, w1, w2, w3, w4, raw, rawc, wet, sea, cor, cmask,
    send_rows, send_strip, recv_rows, recv_strip, sum_sec, sum_lat, got_sec, got_lat,
    halo_send, halo_recv, sec_send, sec_recv, lat_send, lat_recv,
):
    pitch = cols + 2 * HALO
    full = (rows + 2 * HALO) * pitch
    lo, hi = HALO * pitch, (HALO + rows) * pitch
    mid = hi - lo
    sec = lax.axis_index("sec")
    lat = lax.axis_index("lat")

    exists = []
    for dl, ds in DIRS:
        ok = jnp.bool_(True)
        if dl:
            ok = jnp.logical_and(ok, lat > 0 if dl < 0 else lat < n_lat - 1)
        if ds:
            ok = jnp.logical_and(ok, sec > 0 if ds < 0 else sec < n_sec - 1)
        exists.append(ok)

    def peer(dl, ds):
        return {"sec": sec + ds, "lat": lat + dl}

    barrier = pltpu.get_barrier_semaphore()
    for d in range(1, n_sec):
        pl.semaphore_signal(
            barrier, inc=1, device_id={"sec": lax.rem(sec + d, n_sec), "lat": lat},
            device_id_type=pl.DeviceIdType.MESH,
        )
    for d in range(1, n_lat):
        pl.semaphore_signal(
            barrier, inc=1, device_id={"sec": sec, "lat": lax.rem(lat + d, n_lat)},
            device_id_type=pl.DeviceIdType.MESH,
        )
    for k, (dl, ds) in enumerate(DIRS):
        if dl and ds:

            @pl.when(exists[k])
            def _():
                pl.semaphore_signal(
                    barrier, inc=1, device_id=peer(dl, ds), device_id_type=pl.DeviceIdType.MESH
                )

    x[:, full:] = jnp.zeros((4 * LEVELS, x.shape[1] - full), jnp.float32)
    x[:, lo:hi] = xin[...]
    for k in range(len(DIRS)):

        @pl.when(jnp.logical_not(exists[k]))
        def _():
            for t in range(STEPS):
                if k < 2:
                    recv_rows[t, k] = jnp.zeros(recv_rows.shape[2:], jnp.bfloat16)
                else:
                    recv_strip[t, k - 2] = jnp.zeros(recv_strip.shape[2:], jnp.bfloat16)

    n_diag = jnp.int32(0)
    for k, (dl, ds) in enumerate(DIRS):
        if dl and ds:
            n_diag = n_diag + jnp.where(exists[k], 1, 0)
    pl.semaphore_wait(barrier, n_sec - 1 + n_lat - 1 + n_diag)

    lane = lax.broadcasted_iota(jnp.int32, (4 * LEVELS, LANES), 1)

    def halo_copy(t, k):
        dl, ds = DIRS[k]
        back = DIRS.index((-dl, -ds))
        if ds == 0:
            start = 0 if dl < 0 else mid - HALO * pitch
            src = send_rows.at[t, :, start : start + HALO * pitch]
            dst = recv_rows.at[t, back]
        else:
            src = send_strip.at[t, 0 if ds < 0 else 1]
            dst = recv_strip.at[t, back - 2]
        return pltpu.make_async_remote_copy(
            src_ref=src, dst_ref=dst, send_sem=halo_send.at[t, k], recv_sem=halo_recv.at[t, back],
            device_id=peer(dl, ds), device_id_type=pl.DeviceIdType.MESH,
        )

    def halo_arrival(t, k):
        dl, ds = DIRS[k]
        if ds == 0:
            src, dst = send_rows.at[t, :, 0 : HALO * pitch], recv_rows.at[t, k]
        else:
            src, dst = send_strip.at[t, 0], recv_strip.at[t, k - 2]
        return pltpu.make_async_remote_copy(
            src_ref=src, dst_ref=dst, send_sem=halo_send.at[t, k], recv_sem=halo_recv.at[t, k],
            device_id=peer(dl, ds), device_id_type=pl.DeviceIdType.MESH,
        )

    def start_halo(t):
        send_rows[t] = x[:, lo:hi].astype(jnp.bfloat16)
        for side in range(2):
            packed = jnp.zeros((4 * LEVELS, LANES), jnp.float32)
            for row in range(rows):
                place = (HALO + row) * pitch + (HALO if side == 0 else cols)
                base, off = place // LANES * LANES, place % LANES
                part = x[:, base : base + LANES]
                turn = (HALO * row - off) % LANES
                if turn:
                    part = pltpu.roll(part, turn, 1)
                here = (lane >= HALO * row) & (lane < HALO * (row + 1))
                packed = jnp.where(here, part, packed)
            send_strip[t, side] = packed.astype(jnp.bfloat16)
        for k in range(len(DIRS)):

            @pl.when(exists[k])
            def _():
                halo_copy(t, k).start()

    def finish_halo(t):
        for k in range(len(DIRS)):

            @pl.when(exists[k])
            def _():
                halo_arrival(t, k).wait_recv()
                halo_copy(t, k).wait_send()

        x[:, :lo] = recv_rows[t, 0].astype(jnp.float32)
        x[:, hi:full] = recv_rows[t, 1].astype(jnp.float32)
        for side in range(2):
            strips = [recv_strip[t, 3 * side + j].astype(jnp.float32) for j in range(3)]
            for ext in range(rows + 2 * HALO):
                if ext < HALO:
                    strip, from_row = strips[0], rows - HALO + ext
                elif ext < HALO + rows:
                    strip, from_row = strips[1], ext - HALO
                else:
                    strip, from_row = strips[2], ext - HALO - rows
                place = ext * pitch + (0 if side == 0 else HALO + cols)
                base, off = place // LANES * LANES, place % LANES
                turn = (off - HALO * from_row) % LANES
                if turn:
                    strip = pltpu.roll(strip, turn, 1)
                here = (lane >= off) & (lane < off + HALO)
                x[:, base : base + LANES] = jnp.where(here, strip, x[:, base : base + LANES])

    def total(t, mine):
        for axis, count, held, got, send, recv in (
            ("sec", n_sec, sum_sec, got_sec, sec_send, sec_recv),
            ("lat", n_lat, sum_lat, got_lat, lat_send, lat_recv),
        ):
            held[t] = mine
            copies = []
            for d in range(1, count):
                if axis == "sec":
                    target = {"sec": lax.rem(sec + d, count), "lat": lat}
                else:
                    target = {"sec": sec, "lat": lax.rem(lat + d, count)}
                copies.append(
                    pltpu.make_async_remote_copy(
                        src_ref=held.at[t], dst_ref=got.at[t, d - 1], send_sem=send.at[t, d - 1],
                        recv_sem=recv.at[t, d - 1], device_id=target,
                        device_id_type=pl.DeviceIdType.MESH,
                    )
                )
            for copy in copies:
                copy.start()
            for d, copy in enumerate(copies):
                copy.wait_recv()
                mine = mine + got[t, d]
            for copy in copies:
                copy.wait_send()
        counts = jnp.maximum(mine[2 * LEVELS :], 1.0)
        return (mine[: 2 * LEVELS] / jnp.concatenate([counts, counts], axis=0))[:, :1]

    def at(value, offset):
        size = value.shape[1]
        return pltpu.roll(value, (-offset) % size, 1)

    def shifted(ref, count, start, offset, size):
        if offset == 0:
            return ref[:count, pl.ds(pl.multiple_of(start, LANES), size)]
        wide = ref[:count, pl.ds(pl.multiple_of(start, LANES), size + LANES)]
        return at(wide, offset)[:, :size]

    def band(wide, target, depth, width):
        group = target.shape[1] // width
        target[...] = jnp.zeros(target.shape, target.dtype)
        for j in range(group):
            here = slice(j * width, (j + 1) * width)
            for r in range(5):
                q = j + r
                target[q * depth : (q + 1) * depth, here] = wide[r * depth : (r + 1) * depth, here]

    def cells(row, offset=0, count=pitch):
        start = pl.multiple_of(row * pitch, 16)
        return pl.ds(start + offset if offset else start, count)

    def product(source, weight, row):
        depth = source.shape[1]
        parts = [source[cells(row + q), :] for q in range(weight.shape[0] // depth)]
        return jnp.dot(
            jnp.concatenate(parts, axis=1), weight[...], preferred_element_type=jnp.float32
        )

    def silu(value):
        half = 0.5 * value
        return half + half * jnp.tanh(half)

    def sea_row(layer, row):
        return sea[cells(row + 2 * layer, 2 * layer), :]

    def loop(count, body, several):
        several = several if count % several == 0 else 1

        def some(i, carry):
            for j in range(several):
                body(i * several + j, carry)
            return carry

        lax.fori_loop(0, count // several, some, 0)

    lane_of = lax.broadcasted_iota(jnp.int32, (pitch, LANES), 1)

    def network():
        def gather1(i, carry):
            start = i * CHUNK
            parts = [shifted(x, 3 * LEVELS, start, s, CHUNK) for s in range(5)]
            parts.append(jnp.zeros((LANES - 15 * LEVELS, CHUNK), jnp.float32))
            stacked = jnp.concatenate(parts, axis=0)
            s1[pl.ds(pl.multiple_of(start, LANES), CHUNK), :] = stacked.T.astype(jnp.bfloat16)
            return carry

        lax.fori_loop(0, s1.shape[0] // CHUNK, gather1, 0)

        def conv1(g, carry):
            row = 2 * g
            value = silu(product(s1, w1, row) + b1[...])
            for j in range(2):
                a1[cells(row + j), :] = value[:, j * LANES : (j + 1) * LANES] * sea_row(1, row + j)
            return carry

        loop((rows + 12) // 2, conv1, 2)

        def gather2(row, carry):
            for s in range(5):
                s2[cells(row), s * LANES : (s + 1) * LANES] = a1[cells(row, s), :].astype(
                    jnp.bfloat16
                )
            return carry

        loop(rows + 12, gather2, 2)

        def conv2(g, carry):
            row = 4 * g
            value = silu(product(s2, w2, row) + b2[...])
            low = lane_of < LANES // 2
            for k in range(2):
                both = value[:, k * LANES : (k + 1) * LANES]
                turned = pltpu.roll(both, LANES // 2, 1)
                first, second = row + 2 * k, row + 2 * k + 1
                a2[cells(first), :] = jnp.where(low, both, turned) * sea_row(2, first)
                a2[cells(second), :] = jnp.where(low, turned, both) * sea_row(2, second)
            return carry

        loop((rows + 8) // 4, conv2, 2)

        def gather3(row, carry):
            low = lane_of < LANES // 2
            taps = [a2[cells(row, s), :] for s in range(5)]
            pieces = [
                jnp.where(low, taps[0], taps[1]), jnp.where(low, taps[2], taps[3]), taps[4],
            ]
            for k, piece in enumerate(pieces):
                s3[cells(row), k * LANES : (k + 1) * LANES] = piece.astype(jnp.bfloat16)
            return carry

        loop(rows + 8, gather3, 2)

        def conv3(g, carry):
            row = 4 * g
            value = silu(product(s3, w3, row) + b3[...])
            for j in range(4):
                mine = (lane_of >= 32 * j) & (lane_of < 32 * (j + 1))
                one = jnp.where(mine, value, 0.0)
                two = one + pltpu.roll(one, 32, 1)
                four = two + pltpu.roll(two, 64, 1)
                a3[cells(row + j), :] = four * sea_row(3, row + j)
            return carry

        loop((rows + 4) // 4, conv3, 5)

        def gather4(row, carry):
            taps = [a3[cells(row, s), :] for s in range(5)]
            piece = taps[3]
            for j in range(3):
                piece = jnp.where((lane_of >= 32 * j) & (lane_of < 32 * (j + 1)), taps[j], piece)
            s4[cells(row), :LANES] = piece.astype(jnp.bfloat16)
            s4[cells(row), LANES:] = taps[4].astype(jnp.bfloat16)
            return carry

        loop(rows + 4, gather4, 2)

        value = product(s4, w4, 0)
        tall = round_up(pitch, LANES)
        value = jnp.concatenate(
            [value, jnp.zeros((tall - pitch, value.shape[1]), jnp.float32)], axis=0
        ).T
        spot = lax.broadcasted_iota(jnp.int32, (2 * LEVELS, tall), 1)
        for row in range(rows):
            place = row * pitch + HALO
            base, off = place // LANES * LANES, place % LANES
            part = value[row * 2 * LEVELS : (row + 1) * 2 * LEVELS]
            if off:
                part = pltpu.roll(part, off, 1)
            here = (spot >= off) & (spot < off + cols)
            raw[:, base : base + tall] = jnp.where(here, part, raw[:, base : base + tall])

    band(w1_wide, w1, LANES, LANES)
    band(w2_wide, w2, 5 * LANES, LANES // 2)
    band(w3_wide, w3, 3 * LANES, LANES // 4)
    band(w4_wide, w4, 2 * LANES, 2 * LEVELS)
    raw[...] = jnp.zeros(raw.shape, jnp.float32)

    def places():
        spot = lax.broadcasted_iota(jnp.int32, (LEVELS, mid), 1)
        row = jnp.zeros((LEVELS, mid), jnp.int32)
        for k in range(1, rows):
            row = row + jnp.where(spot >= k * pitch, 1, 0)
        col = spot - row * pitch
        global_row = (lat * rows + row).astype(jnp.float32)
        cor[...] = 0.3 + 0.5 * global_row / (n_lat * rows)
        cmask[...] = jnp.where((col >= HALO) & (col < HALO + cols), 1.0, 0.0)

    places()

    def step(t, mine):
        start_halo(t)
        mean = total(t, mine)
        finish_halo(t)

        @pl.when(t == 0)
        def _():
            levels = x[3 * LEVELS :, :full]
            index = lax.broadcasted_iota(jnp.int32, (LEVELS, full), 0).astype(jnp.float32)
            wet[...] = jnp.where(index < levels, 1.0, 0.0)
            sea_here = jnp.where(levels > 0, 1.0, 0.0)
            for start in range(0, full, LANES):
                tile = jnp.concatenate([sea_here[:, start : start + LANES]] * 16, axis=0)
                sea[start : start + LANES, :] = tile.T

        for f in range(2):
            part = slice(f * LEVELS, (f + 1) * LEVELS)
            x[part, :full] = (x[part, :full] - time_step * mean[part]) * wet[...]
        x[2 * LEVELS : 3 * LEVELS, :full] = x[2 * LEVELS : 3 * LEVELS, :full] * wet[...]

        network()

        zonal, merid = x[:LEVELS, :full], x[LEVELS : 2 * LEVELS, :full]
        divergence = (at(zonal, 1) - at(zonal, -1)) * 0.5 + (
            at(merid, pitch) - at(merid, -pitch)
        ) * 0.5
        thick = (x[2 * LEVELS : 3 * LEVELS, :full] - time_step * divergence) * wet[...]
        level = lax.broadcasted_iota(jnp.int32, (LEVELS, 1), 0)
        pressure = jnp.zeros((LEVELS, full), jnp.float32)
        for j in range(LEVELS):
            coef = 0.5 + 0.1 * jnp.minimum(level, j).astype(jnp.float32)
            pressure = pressure + coef * thick[j : j + 1]
        grad_x = ((at(pressure, 1) - at(pressure, -1)) * 0.5)[:, lo:hi]
        grad_y = ((at(pressure, pitch) - at(pressure, -pitch)) * 0.5)[:, lo:hi]
        wet_mid = wet[:, lo:hi]
        zonal, merid = zonal[:, lo:hi], merid[:, lo:hi]
        inside = cmask[...] > 0.0
        raw_u = jnp.where(inside, raw[:LEVELS, :mid], 0.0)
        raw_v = jnp.where(inside, raw[LEVELS:, :mid], 0.0)
        rawc[:LEVELS] = raw_u
        rawc[LEVELS:] = raw_v
        x[:LEVELS, lo:hi] = (
            zonal + time_step * (-grad_x + cor[...] * merid - drag_rate * zonal + raw_u)
        ) * wet_mid
        x[LEVELS : 2 * LEVELS, lo:hi] = (
            merid + time_step * (-grad_y - cor[...] * zonal - drag_rate * merid + raw_v)
        ) * wet_mid
        x[2 * LEVELS : 3 * LEVELS, lo:hi] = thick[:, lo:hi]
        wet_in = jnp.where(inside, wet_mid, 0.0)
        sums = jnp.concatenate(
            [
                jnp.sum(raw_u * wet_in, axis=1, keepdims=True),
                jnp.sum(raw_v * wet_in, axis=1, keepdims=True),
                jnp.sum(wet_in, axis=1, keepdims=True),
            ],
            axis=0,
        )
        return jnp.broadcast_to(sums, (3 * LEVELS, LANES))

    mine = lax.fori_loop(0, STEPS, step, jnp.zeros((3 * LEVELS, LANES), jnp.float32))
    mean = total(STEPS, mine)
    wet_mid = wet[:, lo:hi]
    for f in range(2):
        part = slice(f * LEVELS, (f + 1) * LEVELS)
        state_out[part] = (x[part, lo:hi] - time_step * mean[part]) * wet_mid
        forcing_out[part] = (rawc[part] - mean[part]) * wet_mid
    state_out[2 * LEVELS :] = x[2 * LEVELS : 3 * LEVELS, lo:hi]


def local(
    ocean_state, land_mask, layer_count,
    conv1_weight, conv1_bias, conv2_weight, conv2_bias, conv3_weight, conv3_bias, conv4_weight,
):
    rows, cols = ocean_state.shape[1:]
    n_sec, n_lat = lax.axis_size("sec"), lax.axis_size("lat")
    pitch = cols + 2 * HALO
    full = (rows + 2 * HALO) * pitch
    mid = rows * pitch
    levels = (land_mask * layer_count).astype(jnp.float32)
    fields = jnp.concatenate(
        [ocean_state, jnp.broadcast_to(levels[None], (LEVELS, rows, cols))], axis=0
    )
    xin = jnp.pad(fields, ((0, 0), (0, 0), (HALO, HALO))).reshape(4 * LEVELS, mid)
    def widened(weight, depth, copies):
        turned = weight.transpose(0, 2, 1)
        turned = jnp.pad(turned, ((0, 0), (0, depth - turned.shape[1]), (0, 0)))
        return jnp.tile(turned.reshape(5 * depth, -1), (1, copies))

    w1 = widened(conv1_weight, LANES, 2)
    w2 = widened(conv2_weight, 5 * LANES, 4)
    w3 = widened(conv3_weight, 3 * LANES, 4)
    w4 = widened(conv4_weight, 2 * LANES, rows)
    b1 = jnp.tile(conv1_bias, 2)[None]
    b2 = jnp.tile(conv2_bias, 4)[None]
    b3 = jnp.tile(conv3_bias, 4)[None]
    room = round_up(full, CHUNK) + CHUNK
    bf, f32 = jnp.bfloat16, jnp.float32
    sums = (STEPS + 1, 3 * LEVELS, LANES)
    vmem = pl.BlockSpec(memory_space=pltpu.VMEM)
    state, forcing = pl.pallas_call(
        functools.partial(kernel, rows, cols, n_sec, n_lat),
        out_shape=(
            jax.ShapeDtypeStruct((3 * LEVELS, mid), f32),
            jax.ShapeDtypeStruct((2 * LEVELS, mid), f32),
        ),
        in_specs=[vmem] * 8,
        out_specs=(vmem, vmem),
        scratch_shapes=[
            pltpu.VMEM((4 * LEVELS, room), f32),
            pltpu.VMEM(((rows + 12) * pitch + HALO, LANES), f32),
            pltpu.VMEM(((rows + 8) * pitch + HALO, LANES), f32),
            pltpu.VMEM(((rows + 4) * pitch + HALO, LANES), f32),
            pltpu.VMEM((round_up(full, CHUNK), LANES), bf),
            pltpu.VMEM(((rows + 12) * pitch, 5 * LANES), bf),
            pltpu.VMEM(((rows + 8) * pitch, 3 * LANES), bf),
            pltpu.VMEM(((rows + 4) * pitch, 2 * LANES), bf),
            pltpu.VMEM((6 * LANES, 2 * LANES), bf),
            pltpu.VMEM((8 * 5 * LANES, 2 * LANES), bf),
            pltpu.VMEM((8 * 3 * LANES, LANES), bf),
            pltpu.VMEM(((rows + 4) * 2 * LANES, rows * 2 * LEVELS), bf),
            pltpu.VMEM((2 * LEVELS, mid), f32),
            pltpu.VMEM((2 * LEVELS, mid), f32),
            pltpu.VMEM((LEVELS, full), f32),
            pltpu.VMEM((full, LANES), f32),
            pltpu.VMEM((LEVELS, mid), f32),
            pltpu.VMEM((LEVELS, mid), f32),
            pltpu.VMEM((STEPS, 4 * LEVELS, mid), bf),
            pltpu.VMEM((STEPS, 2, 4 * LEVELS, LANES), bf),
            pltpu.VMEM((STEPS, 2, 4 * LEVELS, HALO * pitch), bf),
            pltpu.VMEM((STEPS, 6, 4 * LEVELS, LANES), bf),
            pltpu.VMEM(sums, f32),
            pltpu.VMEM(sums, f32),
            pltpu.VMEM((STEPS + 1, n_sec - 1) + sums[1:], f32),
            pltpu.VMEM((STEPS + 1, n_lat - 1) + sums[1:], f32),
            pltpu.SemaphoreType.DMA((STEPS, len(DIRS))),
            pltpu.SemaphoreType.DMA((STEPS, len(DIRS))),
            pltpu.SemaphoreType.DMA((STEPS + 1, n_sec - 1)),
            pltpu.SemaphoreType.DMA((STEPS + 1, n_sec - 1)),
            pltpu.SemaphoreType.DMA((STEPS + 1, n_lat - 1)),
            pltpu.SemaphoreType.DMA((STEPS + 1, n_lat - 1)),
        ],
        compiler_params=pltpu.CompilerParams(
            collective_id=0, has_side_effects=True, vmem_limit_bytes=60 * 2**20
        ),
    )(
        xin,
        w1, b1, w2, b2, w3, b3, w4,
    )

    def block(flat):
        return flat.reshape(-1, rows, pitch)[:, :, HALO : HALO + cols]

    return (block(state), block(forcing))


def solution(mesh):
    return jax.shard_map(
        local,
        mesh=mesh,
        in_specs=(
            P(None, "lat", "sec"), P("lat", "sec"), P("lat", "sec"),
            P(), P(), P(), P(), P(), P(), P(),
        ),
        out_specs=(P(None, "lat", "sec"), P(None, "lat", "sec")),
        check_vma=False,
    )
```
